32 devices in a mesh: group: 2 (over x), inst: 2 (over core), tp: 8 (over z, y).
Axes of the slice: x: 2, y: 2, z: 4, core: 2. Of those that a mesh axis runs over, the one named last changes fastest.
Arguments:
- hidden: bfloat16 [2, 256, 8192], P(None, ('group', 'inst', 'tp')), parts along dimension 1, may hold values from -140 to 140
- norm_gain: float32 [2, 8192], replicated, may hold values from 0.1 to 1.9
- kv_weight: bfloat16 [2, 2048, 8192], P(None, 'tp'), may hold values from -0.0625 to 0.0625
- kv_bias: float32 [2, 2048], P(None, 'tp'), may hold values from -3 to 3
- block_request: int32 [32], P(('group', 'inst', 'tp')), parts along dimension 0, may hold values from 0 to 3, never falling along the last dimension, each value on 1 to 8 neighbouring positions
- request_dest: int32 [8], P('group'), parts along dimension 0, may hold values from 0 to 1
- block_slot: int32 [32], P(('group', 'inst', 'tp')), parts along dimension 0, may hold values from 0 to 15, each once
- positions: int32 [256], P(('group', 'inst', 'tp')), parts along dimension 0, may hold values from 0 to 32767
Outputs:
- kv_cache: bfloat16 [2, 64, 8, 2048], P(None, ('group', 'inst'), 'tp'), parts along dimension 1
The draws below stay inside these ranges and needn't reach their ends.
There are 2 independent parts, one for each index of `group`. The reference program is written for one: setup_inputs(seed, part) draws one part's arguments, and reference() takes and returns one part's arrays. A program takes and returns all parts, laid end to end along the dimension named above; an argument that names none is the same for every part. Nothing has to cross between parts.
All inputs are finite; a program needn't handle non-finite values.
Results may differ from the reference program's by a relative error of at most 0.0047.
Values may be sent and summed in bfloat16 or wider, within the bound.
A program may use at most 64 MiB of HBM per device.

```python
import math
import jax
import jax.numpy as jnp
import numpy as np
from jax import lax

D = 8192
HD = 128
LAYERS = 2
PAGE = 8
BLOCKS = 16
TOKENS = 128
REQUESTS = 4
KVW = 2048
COLS_DEV = 256
CACHE_PAGES = 32
N_INST = 2
N_TP = 8


def draw_hidden(key, part):
    key = jax.random.fold_in(key, 11)
    key_base, key_rows, key_cols = jax.random.split(key, 3)
    shape = (LAYERS, TOKENS, D)
    base = jnp.clip(jax.random.normal(key_base, shape, jnp.float32), -4.0, 4.0)
    rows = jnp.exp(jax.random.uniform(key_rows, (LAYERS, TOKENS, 1), jnp.float32, 0.0, math.log(10.0)))
    cols = jnp.exp(jax.random.uniform(key_cols, (LAYERS, 1, D), jnp.float32, 0.0, math.log(10.0)))
    return (base * rows * cols / 3.0).astype(jnp.bfloat16)


def set_ends(array, stream_key, smallest, largest):
    longest = array.shape.index(max(array.shape))
    spots = []
    for shift in (0, 1):
        where = [jax.random.randint(jax.random.fold_in(stream_key, axis), (), 0, length) for axis, length in enumerate(array.shape)]
        where[longest] = (where[longest] + shift) % array.shape[longest]
        spots.append(tuple(where))
    return array.at[spots[0]].set(smallest).at[spots[1]].set(largest)


def levels(stream_key, dims, pieces, smallest, high):
    level, own = 1.0, jax.random.fold_in(stream_key, 6)
    for dim, shards_of in pieces:
        draws = jnp.exp(jax.random.uniform(jax.random.fold_in(own, dim), (shards_of,), jnp.float32, smallest / len(pieces), high / len(pieces)))
        level = level * jnp.repeat(draws, dims[dim] // shards_of).reshape([-1 if axis == dim else 1 for axis in range(len(dims))])
    return level


def profile(amount, total, bound, skew):
    portions = [(1 << 20) // math.isqrt(rank ** skew) + 1 for rank in range(2, amount + 1)]
    rest, given = total - bound - (amount - 1), [1] * (amount - 1)
    while rest > 0:
        candidates = [i for i in range(amount - 1) if given[i] < bound]
        pool, budget = sum([portions[i] for i in candidates]), rest
        for i in candidates:
            extra = min(bound - given[i], max(1, budget * portions[i] // pool), rest)
            given[i] = given[i] + extra
            rest = rest - extra
    return np.array([bound] + given)


def ragged_sizes(own_key, number_of, total, bound, lean):
    if number_of == 2:
        one = jax.random.randint(own_key, (), max(1, total - bound), min(bound, total - 1) + 1)
        return jnp.stack([one, total - one])
    tallies = jnp.asarray(profile(number_of, total, bound, lean), jnp.int32)
    twos = (number_of - 1) // 2
    giver, receiver = tallies[1:1 + 2 * twos:2], tallies[2:2 + 2 * twos:2]
    slack = jnp.minimum(giver - 1, bound - receiver)
    moved = jax.random.randint(jax.random.fold_in(own_key, 1), (twos,), 0, 1 << 20) % (slack + 1)
    tallies = tallies.at[1:1 + 2 * twos:2].set(giver - moved).at[2:2 + 2 * twos:2].set(receiver + moved)
    return tallies[jax.random.permutation(jax.random.fold_in(own_key, 2), number_of)]


def noise(rng, extent, width, limit, cuts=(), kind=jnp.bfloat16):
    values = width * jax.random.normal(rng, extent, jnp.float32)
    if cuts:
        values = values * levels(rng, extent, cuts, -0.22, 0.18)
    return jnp.clip(values, -limit, limit).astype(kind)


def setup_inputs(seed: int = 0, part: int = 0) -> dict:
    key_list = jax.random.split(jax.random.key(seed), 9)
    own_keys = jax.random.split(jax.random.fold_in(key_list[8], part), 9)
    hidden = draw_hidden(jax.random.fold_in(jax.random.fold_in(key_list[8], part), 71), part)
    norm_gain = jnp.clip(1.0 + 0.18 * jax.random.normal(key_list[1], (LAYERS, D), jnp.float32), 0.1, 1.9)
    kv_weight = noise(key_list[2], (LAYERS, KVW, D), D ** -0.5, 0.0625, ((1, 8),))
    kv_bias = noise(key_list[3], (LAYERS, KVW), 0.5, 3.0, ((1, 8),), jnp.float32)
    block_request = jnp.searchsorted(jnp.cumsum(ragged_sizes(own_keys[4], REQUESTS, BLOCKS, 8, 0)), jnp.arange(BLOCKS), side="right").astype(jnp.int32)
    request_dest = set_ends(jax.random.randint(own_keys[5], (REQUESTS,), 0, N_INST), jax.random.fold_in(own_keys[5], 1), 0, N_INST - 1).astype(jnp.int32)
    block_slot = jax.random.permutation(own_keys[6], BLOCKS).astype(jnp.int32)
    positions = set_ends(jax.random.randint(own_keys[7], (TOKENS,), 0, 32768), jax.random.fold_in(own_keys[7], 1), 0, 32767).astype(jnp.int32)
    return {"hidden": hidden, "norm_gain": norm_gain, "kv_weight": kv_weight, "kv_bias": kv_bias, "block_request": block_request, "request_dest": request_dest, "block_slot": block_slot, "positions": positions}


EPSILON = 1e-06
ROPE_BASE = 1000000.0

def rotary_parts(columns):
    freq_idx = columns % HD // 2
    inv_freq = jnp.exp(-(2.0 * freq_idx.astype(jnp.float32) / HD) * math.log(ROPE_BASE))
    is_key = columns % (2 * HD) < HD
    return (inv_freq, is_key)

def project(hidden_rows, gain_row, weight, bias_row, places, inv_freq, is_key):
    values_f = hidden_rows.astype(jnp.float32)
    inv_rms = lax.rsqrt(lax.optimization_barrier(jnp.mean(values_f * values_f, axis=-1, keepdims=True)) + EPSILON)
    normed = (values_f * inv_rms * gain_row).astype(jnp.bfloat16)
    projected = lax.dot_general(normed, weight, (((1,), (1,)), ((), ())), preferred_element_type=jnp.float32) + bias_row
    angles = places[:, None].astype(jnp.float32) * inv_freq[None, :]
    paired = projected.reshape(projected.shape[0], -1, 2)
    partner = jnp.stack([-paired[:, :, 1], paired[:, :, 0]], axis=-1).reshape(projected.shape)
    turned = projected * jnp.cos(angles) + partner * jnp.sin(angles)
    return jnp.where(is_key[None, :], turned, projected).astype(jnp.bfloat16)

def reference(hidden, norm_gain, kv_weight, kv_bias, block_request, request_dest, block_slot, positions):
    block_dest = request_dest[block_request].astype(jnp.int32)
    target = (block_dest * BLOCKS + block_slot).astype(jnp.int32)
    columns = jnp.arange(KVW, dtype=jnp.int32)
    inv_freq, is_key = rotary_parts(columns)
    caches = []
    for layer_idx in range(LAYERS):
        rotated = project(hidden[layer_idx], norm_gain[layer_idx], kv_weight[layer_idx], kv_bias[layer_idx], positions, inv_freq, is_key)
        pages = rotated.reshape(BLOCKS, PAGE, N_TP, COLS_DEV).transpose(0, 2, 1, 3).reshape(BLOCKS, N_TP, PAGE * COLS_DEV)
        caches.append(jnp.zeros((CACHE_PAGES, N_TP, PAGE * COLS_DEV), jnp.bfloat16).at[target].set(pages))
    return jnp.stack(caches)
```

```python
import functools
import math

import jax
import jax.numpy as jnp
from jax import lax
from jax.experimental import pallas as pl
from jax.experimental.pallas import tpu as pltpu
from jax.sharding import PartitionSpec as P

HD = 128
EPSILON = 1e-06
ROPE_BASE = 1000000.0
LOOKAHEAD = 3
MESH = pl.DeviceIdType.MESH
Y, UP, DOWN = 0, 1, 2


def kernel(
    team, chunks, page_len, page_count, slots,
    request_ref, dest_ref, slot_ref, place_ref,
    hidden_hbm, gain_hbm, weight_hbm, bias_hbm,
    out_ref,
    hidden, gain, weight, bias, rows, meta, far_code, total, turned, cos_ref, sin_ref, pick,
    load_sem, send_sem, recv_sem, meta_send, meta_recv, pair_send, pair_recv,
):
    layers, row_count, model_dim = hidden.shape
    width = weight.shape[1]
    wide = total.shape[2]
    depth = model_dim // chunks
    line = team // 2
    inst = lax.axis_index("inst")
    me = lax.axis_index("tp")
    z = me // 2
    y = me % 2
    peer = (me + 1 - 2 * y, me + 2, me - 2)
    has_up = z < line - 1
    has_down = z > 0

    loads = [
        pltpu.make_async_copy(hidden_hbm, hidden, load_sem.at[0]),
        pltpu.make_async_copy(gain_hbm, gain, load_sem.at[1]),
        pltpu.make_async_copy(bias_hbm, bias, load_sem.at[2]),
        pltpu.make_async_copy(weight_hbm, weight, load_sem.at[3]),
    ]
    for load in loads:
        load.start()

    barrier = pltpu.get_barrier_semaphore()
    pl.semaphore_signal(barrier, inc=1, device_id={"inst": 1 - inst}, device_id_type=MESH)
    pl.semaphore_signal(barrier, inc=1, device_id={"tp": peer[Y]}, device_id_type=MESH)

    @pl.when(has_up)
    def _():
        pl.semaphore_signal(barrier, inc=1, device_id={"tp": peer[UP]}, device_id_type=MESH)

    @pl.when(has_down)
    def _():
        pl.semaphore_signal(barrier, inc=1, device_id={"tp": peer[DOWN]}, device_id_type=MESH)

    sub = lax.broadcasted_iota(jnp.int32, (row_count, 128), 0)
    place = jnp.zeros((row_count, 128), jnp.int32)
    code = jnp.zeros((row_count, 128), jnp.int32)
    for r in range(row_count):
        place = jnp.where(sub == r, place_ref[r], place)
    for b in range(page_count):
        dest = jnp.int32(0)
        for q in range(dest_ref.shape[0]):
            dest = dest + jnp.where(request_ref[b] == q, dest_ref[q], 0)
        code = jnp.where(sub // page_len == b, dest * slots + slot_ref[b], code)
    meta[me, 0] = place
    meta[me, 1] = code

    loads[0].wait()
    loads[1].wait()
    inv_rms = []
    for layer in range(layers):
        square = jnp.zeros((row_count, 128), jnp.float32)
        for j in range(model_dim // 128):
            values = hidden[layer, :, j * 128:(j + 1) * 128].astype(jnp.float32)
            square = square + values * values
        mean = jnp.sum(square, axis=1, keepdims=True) * (1.0 / model_dim)
        inv_rms.append(lax.rsqrt(mean + EPSILON))

    pl.semaphore_wait(barrier, 2 + has_up.astype(jnp.int32) + has_down.astype(jnp.int32))

    def copies(c, block, way):
        made = [
            pltpu.make_async_remote_copy(
                src_ref=rows.at[c, block], dst_ref=rows.at[c, block],
                send_sem=send_sem.at[way, c, block], recv_sem=recv_sem.at[c, block],
                device_id={"tp": peer[way]}, device_id_type=MESH,
            )
        ]
        if c == 0:
            made.append(
                pltpu.make_async_remote_copy(
                    src_ref=meta.at[block], dst_ref=meta.at[block],
                    send_sem=meta_send.at[way, block], recv_sem=meta_recv.at[block],
                    device_id={"tp": peer[way]}, device_id_type=MESH,
                )
            )
        return made

    def send(c, block, way):
        for copy in copies(c, block, way):
            copy.start()

    def receive(c, block):
        for copy in copies(c, block, Y):
            copy.wait_recv()

    def send_own(c):
        span = slice(c * depth, (c + 1) * depth)
        normed = [
            hidden[layer, :, span].astype(jnp.float32) * inv_rms[layer] * gain[layer:layer + 1, span]
            for layer in range(layers)
        ]
        rows[c, me] = jnp.concatenate(normed, axis=0).astype(jnp.bfloat16)
        send(c, me, Y)
        pl.when(has_up)(lambda: send(c, me, UP))
        pl.when(has_down)(lambda: send(c, me, DOWN))

    def forward(c, step):
        low, high = me - 2 * step, me + 2 * step

        @pl.when(z >= step)
        def _():
            receive(c, low)
            send(c, low, Y)
            pl.when(has_up)(lambda: send(c, low, UP))

        @pl.when(z + step < line)
        def _():
            receive(c, high)
            send(c, high, Y)
            pl.when(has_down)(lambda: send(c, high, DOWN))

    tokens = team * row_count
    places = page_len * slots

    pair_code = pltpu.make_async_remote_copy(
        src_ref=meta, dst_ref=far_code, send_sem=pair_send.at[0], recv_sem=pair_recv.at[0],
        device_id={"inst": 1 - inst}, device_id_type=MESH,
    )

    def tables():
        position = meta[:, 0].reshape(tokens, 128).astype(jnp.float32)
        for g in range(wide // 128):
            if width % (2 * HD) == 0 and g % 2:
                continue
            column = me * width + g * 128 + lax.broadcasted_iota(jnp.int32, (1, 128), 1)
            freq = (column % HD // 2).astype(jnp.float32)
            angle = position * jnp.exp(-(2.0 * freq / HD) * math.log(ROPE_BASE))
            is_key = column % (2 * HD) < HD
            lanes = slice(g * 128, (g + 1) * 128)
            cos_ref[:, lanes] = jnp.where(is_key, jnp.cos(angle), 1.0)
            sine = jnp.where(is_key, jnp.sin(angle), 0.0)
            sin_ref[:, lanes] = jnp.where(column % 2 == 0, -sine, sine)

    def picks(side, source):
        code = source[:, 1].reshape(tokens, 128)[:, 0:1]
        spot = lax.broadcasted_iota(jnp.int32, (tokens, places), 1)
        token = lax.broadcasted_iota(jnp.int32, (tokens, places), 0)
        hit = (code == inst * slots + spot % slots) & (token % page_len == spot // slots)
        pick[side] = jnp.where(hit, 1.0, 0.0).T.astype(jnp.bfloat16)

    def multiply(c):
        block = rows[c].reshape(team * layers * row_count, depth)
        for layer in range(layers):
            part = lax.dot_general(
                block, weight[layer, :, c * depth:(c + 1) * depth],
                (((1,), (1,)), ((), ())), preferred_element_type=jnp.float32,
            )
            if c == 0:
                total[layer, :, :width] = part
            else:
                total[layer, :, :width] += part

    if wide != width:
        total[...] = jnp.zeros_like(total)
    for c in range(min(LOOKAHEAD, chunks)):
        send_own(c)
    for wave in range(chunks + line):
        if wave + LOOKAHEAD < chunks:
            send_own(wave + LOOKAHEAD)
        for step in range(1, line):
            if 0 <= wave - step < chunks:
                forward(wave - step, step)
        c = wave - line
        if 0 <= c < chunks:
            for far in range(line):
                receive(c, 2 * far + 1 - y)
            if c == 0:
                pair_code.start()
                loads[2].wait()
                loads[3].wait()
                tables()
                picks(0, meta)
            multiply(c)
    pair_code.wait_recv()
    picks(1, far_code)

    lane = lax.broadcasted_iota(jnp.int32, (1, 128), 1)
    for layer in range(layers):
        acc = total[layer].reshape(team, layers * row_count, wide)
        acc = acc[:, layer * row_count:(layer + 1) * row_count].reshape(tokens, wide)
        for g in range(wide // 128):
            start, end = g * 128, min((g + 1) * 128, width)
            value = acc[:, g * 128:(g + 1) * 128]
            shift = bias[layer:layer + 1, start:end]
            if end - start < 128:
                shift = jnp.pad(shift, ((0, 0), (0, 128 - (end - start))))
            value = value + shift
            if not (width % (2 * HD) == 0 and g % 2):
                after = pltpu.roll(value, 127, 1)
                before = pltpu.roll(value, 1, 1)
                partner = jnp.where(lane % 2 == 0, after, before)
                value = value * cos_ref[:, start:start + 128] + partner * sin_ref[:, start:start + 128]
            turned[0, layer, :, g * 128:(g + 1) * 128] = value.astype(jnp.bfloat16)

    swap = pltpu.make_async_remote_copy(
        src_ref=turned.at[0], dst_ref=turned.at[1], send_sem=pair_send.at[1], recv_sem=pair_recv.at[1],
        device_id={"inst": 1 - inst}, device_id_type=MESH,
    )
    swap.start()
    near = [
        jnp.dot(pick[0], turned[0, layer], preferred_element_type=jnp.float32) for layer in range(layers)
    ]
    swap.wait_recv()
    for layer in range(layers):
        paged = near[layer] + jnp.dot(pick[1], turned[1, layer], preferred_element_type=jnp.float32)
        paged = paged.astype(jnp.bfloat16)
        for r in range(page_len):
            page_rows = paged[r * slots:(r + 1) * slots]
            if out_ref.ndim == 3:
                out_ref[layer, :, r * width:(r + 1) * width] = page_rows
            else:
                out_ref[layer, r] = page_rows

    def sent(c, block, way):
        for copy in copies(c, block, way):
            copy.wait_send()

    pair_code.wait_send()
    swap.wait_send()
    for c in range(chunks):
        sent(c, me, Y)
        pl.when(has_up)(functools.partial(sent, c, me, UP))
        pl.when(has_down)(functools.partial(sent, c, me, DOWN))
        for step in range(1, line):
            low, high = me - 2 * step, me + 2 * step

            @pl.when(z >= step)
            def _():
                sent(c, low, Y)
                pl.when(has_up)(functools.partial(sent, c, low, UP))

            @pl.when(z + step < line)
            def _():
                sent(c, high, Y)
                pl.when(has_down)(functools.partial(sent, c, high, DOWN))


def body(hidden, norm_gain, kv_weight, kv_bias, block_request, request_dest, block_slot, positions):
    layers, row_count, model_dim = hidden.shape
    page_count = block_request.shape[0]
    page_len = row_count // page_count
    width = kv_weight.shape[1]
    inst_count = lax.axis_size("inst")
    team = lax.axis_size("tp")
    slots = inst_count * team * page_count
    wide = -(-width // 128) * 128
    chunks = max(1, 64 // team)
    depth = model_dim // chunks
    tokens = team * row_count
    line = team // 2
    if wide == width:
        shape = (layers, slots, page_len * width)
    else:
        shape = (layers, page_len, slots, wide)
    smem = pl.BlockSpec(memory_space=pltpu.SMEM)
    anywhere = pl.BlockSpec(memory_space=pl.ANY)
    dma = pltpu.SemaphoreType.DMA
    out = pl.pallas_call(
        functools.partial(kernel, team, chunks, page_len, page_count, slots),
        out_shape=jax.ShapeDtypeStruct(shape, jnp.bfloat16),
        in_specs=[smem] * 4 + [anywhere] * 4,
        out_specs=pl.BlockSpec(memory_space=pltpu.VMEM),
        scratch_shapes=[
            pltpu.VMEM((layers, row_count, model_dim), jnp.bfloat16),
            pltpu.VMEM((layers, model_dim), jnp.float32),
            pltpu.VMEM((layers, width, model_dim), jnp.bfloat16),
            pltpu.VMEM((layers, width), jnp.float32),
            pltpu.VMEM((chunks, team, layers * row_count, depth), jnp.bfloat16),
            pltpu.VMEM((team, 2, row_count, 128), jnp.int32),
            pltpu.VMEM((team, 2, row_count, 128), jnp.int32),
            pltpu.VMEM((layers, team * layers * row_count, wide), jnp.float32),
            pltpu.VMEM((2, layers, tokens, wide), jnp.bfloat16),
            pltpu.VMEM((tokens, wide), jnp.float32),
            pltpu.VMEM((tokens, wide), jnp.float32),
            pltpu.VMEM((2, page_len * slots, tokens), jnp.bfloat16),
            dma((4,)),
            dma((3, chunks, team)),
            dma((chunks, team)),
            dma((3, team)),
            dma((team,)),
            dma((2,)),
            dma((2,)),
        ],
        compiler_params=pltpu.CompilerParams(
            collective_id=0, has_side_effects=True, vmem_limit_bytes=48 * 1024 * 1024
        ),
        cost_estimate=pl.CostEstimate(
            flops=4 * layers * tokens * width * model_dim,
            bytes_accessed=2 * layers * width * model_dim,
            transcendentals=0,
        ),
        name="restore",
    )(block_request, request_dest, block_slot, positions, hidden, norm_gain, kv_weight, kv_bias)
    if wide != width:
        out = out[..., :width].transpose(0, 2, 1, 3)
    return out.reshape(layers, slots, 1, page_len * width)


def solution(mesh):
    placed = (
        P(None, ("group", "inst", "tp"), None),
        P(),
        P(None, "tp", None),
        P(None, "tp"),
        P(("group", "inst", "tp")),
        P("group"),
        P(("group", "inst", "tp")),
        P(("group", "inst", "tp")),
    )
    return jax.shard_map(
        body,
        mesh=mesh,
        in_specs=placed,
        out_specs=P(None, ("group", "inst"), "tp", None),
        check_vma=False,
    )
```

```python
import functools
import math

import jax
import jax.numpy as jnp
from jax import lax
from jax.experimental import pallas as pl
from jax.experimental.pallas import tpu as pltpu
from jax.sharding import PartitionSpec as P

HD = 128
EPSILON = 1e-06
ROPE_BASE = 1000000.0
LOOKAHEAD = 8
MESH = pl.DeviceIdType.MESH
GAP = 2
Y, UP, DOWN = 0, 1, 2


def kernel(
    team, chunks, crossed, page_len, page_count, slots,
    request_ref, dest_ref, slot_ref, place_ref,
    hidden_hbm, gain_hbm, weight_hbm, bias_hbm,
    out_ref,
    hidden, gain, weight, bias, rows, meta, far_code, total, turned, cos_ref, sin_ref, pick,
    load_sem, send_sem, recv_sem, meta_send, meta_recv, pair_send, pair_recv,
):
    layers, row_count, model_dim = hidden.shape
    width = weight.shape[1]
    wide = total.shape[2]
    depth = model_dim // chunks
    line = team // 2
    inst = lax.axis_index("inst")
    me = lax.axis_index("tp")
    z = me // 2
    y = me % 2
    peer = (me + 1 - 2 * y, me + 2, me - 2)
    has_up = z < line - 1
    has_down = z > 0

    loads = [
        pltpu.make_async_copy(hidden_hbm, hidden, load_sem.at[0]),
        pltpu.make_async_copy(gain_hbm, gain, load_sem.at[1]),
        pltpu.make_async_copy(bias_hbm, bias, load_sem.at[2]),
        pltpu.make_async_copy(weight_hbm, weight, load_sem.at[3]),
    ]
    for load in loads:
        load.start()

    barrier = pltpu.get_barrier_semaphore()
    pl.semaphore_signal(barrier, inc=1, device_id={"inst": 1 - inst}, device_id_type=MESH)
    pl.semaphore_signal(barrier, inc=1, device_id={"tp": peer[Y]}, device_id_type=MESH)

    @pl.when(has_up)
    def _():
        pl.semaphore_signal(barrier, inc=1, device_id={"tp": peer[UP]}, device_id_type=MESH)

    @pl.when(has_down)
    def _():
        pl.semaphore_signal(barrier, inc=1, device_id={"tp": peer[DOWN]}, device_id_type=MESH)

    sub = lax.broadcasted_iota(jnp.int32, (row_count, 128), 0)
    place = jnp.zeros((row_count, 128), jnp.int32)
    code = jnp.zeros((row_count, 128), jnp.int32)
    for r in range(row_count):
        place = jnp.where(sub == r, place_ref[r], place)
    for b in range(page_count):
        dest = jnp.int32(0)
        for q in range(dest_ref.shape[0]):
            dest = dest + jnp.where(request_ref[b] == q, dest_ref[q], 0)
        code = jnp.where(sub // page_len == b, dest * slots + slot_ref[b], code)
    meta[me, 0] = place
    meta[me, 1] = code

    loads[0].wait()
    loads[1].wait()
    inv_rms = []
    for layer in range(layers):
        square = jnp.zeros((row_count, 128), jnp.float32)
        for j in range(model_dim // 128):
            values = hidden[layer, :, j * 128:(j + 1) * 128].astype(jnp.float32)
            square = square + values * values
        mean = jnp.sum(square, axis=1, keepdims=True) * (1.0 / model_dim)
        inv_rms.append(lax.rsqrt(mean + EPSILON))

    pl.semaphore_wait(barrier, 2 + has_up.astype(jnp.int32) + has_down.astype(jnp.int32))

    def copies(c, block, way):
        made = [
            pltpu.make_async_remote_copy(
                src_ref=rows.at[c, block], dst_ref=rows.at[c, block],
                send_sem=send_sem.at[way, c, block], recv_sem=recv_sem.at[c, block],
                device_id={"tp": peer[way]}, device_id_type=MESH,
            )
        ]
        if c == 0:
            made.append(
                pltpu.make_async_remote_copy(
                    src_ref=meta.at[block], dst_ref=meta.at[block],
                    send_sem=meta_send.at[way, block], recv_sem=meta_recv.at[block],
                    device_id={"tp": peer[way]}, device_id_type=MESH,
                )
            )
        return made

    def send(c, block, way):
        for copy in copies(c, block, way):
            copy.start()

    def receive(c, block):
        for copy in copies(c, block, Y):
            copy.wait_recv()

    both = ((UP, has_up), (DOWN, has_down))

    def hops(c):
        found = []
        for step in range(1, line):
            low, high = z >= step, z + step < line
            if c < crossed:
                found += [
                    (step, low, me - 2 * step, both[:1]),
                    (step, high, me + 2 * step, both[1:]),
                    (step + 1, low, peer[Y] - 2 * step, both[:1]),
                    (step + 1, high, peer[Y] + 2 * step, both[1:]),
                ]
            else:
                found += [
                    (step, low, me - 2 * step, ((Y, None),) + both[:1]),
                    (step, high, me + 2 * step, ((Y, None),) + both[1:]),
                ]
        if c < crossed:
            found.append((1, None, peer[Y], both))
        return found

    def guarded(cond, act):
        if cond is None:
            act()
        else:
            pl.when(cond)(act)

    def onward(act, c, block, ways):
        for way, cond in ways:
            guarded(cond, functools.partial(act, c, block, way))

    def send_own(c):
        span = slice(c * depth, (c + 1) * depth)
        normed = [
            hidden[layer, :, span].astype(jnp.float32) * inv_rms[layer] * gain[layer:layer + 1, span]
            for layer in range(layers)
        ]
        rows[c, me] = jnp.concatenate(normed, axis=0).astype(jnp.bfloat16)
        onward(send, c, me, ((Y, None),) + both)

    def forward(c, block, ways):
        receive(c, block)
        onward(send, c, block, ways)

    tokens = team * row_count
    places = page_len * slots

    pair_code = pltpu.make_async_remote_copy(
        src_ref=meta, dst_ref=far_code, send_sem=pair_send.at[0], recv_sem=pair_recv.at[0],
        device_id={"inst": 1 - inst}, device_id_type=MESH,
    )

    def tables():
        position = meta[:, 0].reshape(tokens, 128).astype(jnp.float32)
        for g in range(wide // 128):
            if width % (2 * HD) == 0 and g % 2:
                continue
            column = me * width + g * 128 + lax.broadcasted_iota(jnp.int32, (1, 128), 1)
            freq = (column % HD // 2).astype(jnp.float32)
            angle = position * jnp.exp(-(2.0 * freq / HD) * math.log(ROPE_BASE))
            is_key = column % (2 * HD) < HD
            lanes = slice(g * 128, (g + 1) * 128)
            cos_ref[:, lanes] = jnp.where(is_key, jnp.cos(angle), 1.0)
            sine = jnp.where(is_key, jnp.sin(angle), 0.0)
            sin_ref[:, lanes] = jnp.where(column % 2 == 0, -sine, sine)

    def picks(side, source):
        code = source[:, 1].reshape(tokens, 128)[:, 0:1]
        spot = lax.broadcasted_iota(jnp.int32, (tokens, places), 1)
        token = lax.broadcasted_iota(jnp.int32, (tokens, places), 0)
        hit = (code == inst * slots + spot % slots) & (token % page_len == spot // slots)
        pick[side] = jnp.where(hit, 1.0, 0.0).T.astype(jnp.bfloat16)

    def multiply(c, fresh):
        block = rows[c].reshape(team * layers * row_count, depth)
        for layer in range(layers):
            part = lax.dot_general(
                block, weight[layer, :, c * depth:(c + 1) * depth],
                (((1,), (1,)), ((), ())), preferred_element_type=jnp.float32,
            )
            if fresh:
                total[layer, :, :width] = part
            else:
                total[layer, :, :width] += part

    if wide != width:
        total[...] = jnp.zeros_like(total)
    gap = GAP or chunks
    events = []
    for c in range(chunks):
        events.append((max(0, c - LOOKAHEAD), 0, len(events), functools.partial(send_own, c)))
        for stage, cond, block, ways in hops(c):
            act = functools.partial(guarded, cond, functools.partial(forward, c, block, ways))
            events.append((c + gap * stage, 1, len(events), act))

    first = crossed if crossed < chunks else 0

    def finish(c):
        if c >= crossed:
            for far in range(line):
                receive(c, 2 * far + 1 - y)
        if c == first:
            loads[2].wait()
            loads[3].wait()
        multiply(c, c == first)
        if c == 0:
            pair_code.start()
            tables()
            picks(0, meta)
        if c == min(1, chunks - 1):
            pair_code.wait_recv()
            picks(1, far_code)

    for c in range(chunks):
        events.append((max(c + gap * line, c + gap * (line + 1) if c < crossed else 0), 2, len(events), functools.partial(finish, c)))
    for event in sorted(events, key=lambda e: e[:3]):
        event[3]()

    lane = lax.broadcasted_iota(jnp.int32, (1, 128), 1)
    for layer in range(layers):
        acc = total[layer].reshape(team, layers * row_count, wide)
        acc = acc[:, layer * row_count:(layer + 1) * row_count].reshape(tokens, wide)
        for g in range(wide // 128):
            start, end = g * 128, min((g + 1) * 128, width)
            value = acc[:, g * 128:(g + 1) * 128]
            shift = bias[layer:layer + 1, start:end]
            if end - start < 128:
                shift = jnp.pad(shift, ((0, 0), (0, 128 - (end - start))))
            value = value + shift
            if not (width % (2 * HD) == 0 and g % 2):
                after = pltpu.roll(value, 127, 1)
                before = pltpu.roll(value, 1, 1)
                partner = jnp.where(lane % 2 == 0, after, before)
                value = value * cos_ref[:, start:start + 128] + partner * sin_ref[:, start:start + 128]
            turned[0, layer, :, g * 128:(g + 1) * 128] = value.astype(jnp.bfloat16)

    swap = pltpu.make_async_remote_copy(
        src_ref=turned.at[0], dst_ref=turned.at[1], send_sem=pair_send.at[1], recv_sem=pair_recv.at[1],
        device_id={"inst": 1 - inst}, device_id_type=MESH,
    )
    swap.start()
    near = [
        jnp.dot(pick[0], turned[0, layer], preferred_element_type=jnp.float32) for layer in range(layers)
    ]
    swap.wait_recv()
    for layer in range(layers):
        paged = near[layer] + jnp.dot(pick[1], turned[1, layer], preferred_element_type=jnp.float32)
        paged = paged.astype(jnp.bfloat16)
        for r in range(page_len):
            page_rows = paged[r * slots:(r + 1) * slots]
            if out_ref.ndim == 3:
                out_ref[layer, :, r * width:(r + 1) * width] = page_rows
            else:
                out_ref[layer, r] = page_rows

    def sent(c, block, way):
        for copy in copies(c, block, way):
            copy.wait_send()

    pair_code.wait_send()
    swap.wait_send()
    for c in range(chunks):
        onward(sent, c, me, ((Y, None),) + both)
        for _, cond, block, ways in hops(c):
            guarded(cond, functools.partial(onward, sent, c, block, ways))


def body(hidden, norm_gain, kv_weight, kv_bias, block_request, request_dest, block_slot, positions):
    layers, row_count, model_dim = hidden.shape
    page_count = block_request.shape[0]
    page_len = row_count // page_count
    width = kv_weight.shape[1]
    inst_count = lax.axis_size("inst")
    team = lax.axis_size("tp")
    slots = inst_count * team * page_count
    wide = -(-width // 128) * 128
    chunks = max(1, 32 // team)
    depth = model_dim // chunks
    tokens = team * row_count
    line = team // 2
    if wide == width:
        shape = (layers, slots, page_len * width)
    else:
        shape = (layers, page_len, slots, wide)
    smem = pl.BlockSpec(memory_space=pltpu.SMEM)
    anywhere = pl.BlockSpec(memory_space=pl.ANY)
    dma = pltpu.SemaphoreType.DMA
    out = pl.pallas_call(
        functools.partial(kernel, team, chunks, chunks // 8, page_len, page_count, slots),
        out_shape=jax.ShapeDtypeStruct(shape, jnp.bfloat16),
        in_specs=[smem] * 4 + [anywhere] * 4,
        out_specs=pl.BlockSpec(memory_space=pltpu.VMEM),
        scratch_shapes=[
            pltpu.VMEM((layers, row_count, model_dim), jnp.bfloat16),
            pltpu.VMEM((layers, model_dim), jnp.float32),
            pltpu.VMEM((layers, width, model_dim), jnp.bfloat16),
            pltpu.VMEM((layers, width), jnp.float32),
            pltpu.VMEM((chunks, team, layers * row_count, depth), jnp.bfloat16),
            pltpu.VMEM((team, 2, row_count, 128), jnp.int32),
            pltpu.VMEM((team, 2, row_count, 128), jnp.int32),
            pltpu.VMEM((layers, team * layers * row_count, wide), jnp.float32),
            pltpu.VMEM((2, layers, tokens, wide), jnp.bfloat16),
            pltpu.VMEM((tokens, wide), jnp.float32),
            pltpu.VMEM((tokens, wide), jnp.float32),
            pltpu.VMEM((2, page_len * slots, tokens), jnp.bfloat16),
            dma((4,)),
            dma((3, chunks, team)),
            dma((chunks, team)),
            dma((3, team)),
            dma((team,)),
            dma((2,)),
            dma((2,)),
        ],
        compiler_params=pltpu.CompilerParams(
            collective_id=0, has_side_effects=True, vmem_limit_bytes=62 * 1024 * 1024
        ),
        cost_estimate=pl.CostEstimate(
            flops=4 * layers * tokens * width * model_dim,
            bytes_accessed=2 * layers * width * model_dim,
            transcendentals=0,
        ),
        name="restore",
    )(block_request, request_dest, block_slot, positions, hidden, norm_gain, kv_weight, kv_bias)
    if wide != width:
        out = out[..., :width].transpose(0, 2, 1, 3)
    return out.reshape(layers, slots, 1, page_len * width)


def solution(mesh):
    placed = (
        P(None, ("group", "inst", "tp"), None),
        P(),
        P(None, "tp", None),
        P(None, "tp"),
        P(("group", "inst", "tp")),
        P("group"),
        P(("group", "inst", "tp")),
        P(("group", "inst", "tp")),
    )
    return jax.shard_map(
        body,
        mesh=mesh,
        in_specs=placed,
        out_specs=P(None, ("group", "inst"), "tp", None),
        check_vma=False,
    )
```

```python
import functools
import math

import jax
import jax.numpy as jnp
from jax import lax
from jax.experimental import pallas as pl
from jax.experimental.pallas import tpu as pltpu
from jax.sharding import PartitionSpec as P

HD = 128
EPSILON = 1e-06
ROPE_BASE = 1000000.0
LOOKAHEAD = 8
MESH = pl.DeviceIdType.MESH
GAP = 2
Y, UP, DOWN = 0, 1, 2


def kernel(
    team, chunks, crossed, page_len, page_count, slots,
    request_ref, dest_ref, slot_ref, place_ref,
    hidden_hbm, gain_hbm, weight_hbm, bias_hbm,
    out_ref,
    hidden, gain, weight, bias, rows, meta, far_code, total, turned, cos_ref, sin_ref, pick,
    load_sem, send_sem, recv_sem, meta_send, meta_recv, pair_send, pair_recv,
):
    layers, row_count, model_dim = hidden.shape
    width = weight.shape[1]
    wide = total.shape[2]
    depth = model_dim // chunks
    line = team // 2
    inst = lax.axis_index("inst")
    me = lax.axis_index("tp")
    z = me // 2
    y = me % 2
    peer = (me + 1 - 2 * y, me + 2, me - 2)
    has_up = z < line - 1
    has_down = z > 0

    loads = [
        pltpu.make_async_copy(hidden_hbm, hidden, load_sem.at[0]),
        pltpu.make_async_copy(gain_hbm, gain, load_sem.at[1]),
        pltpu.make_async_copy(bias_hbm, bias, load_sem.at[2]),
        pltpu.make_async_copy(weight_hbm, weight, load_sem.at[3]),
    ]
    for load in loads:
        load.start()

    barrier = pltpu.get_barrier_semaphore()
    pl.semaphore_signal(barrier, inc=1, device_id={"inst": 1 - inst}, device_id_type=MESH)
    pl.semaphore_signal(barrier, inc=1, device_id={"tp": peer[Y]}, device_id_type=MESH)

    @pl.when(has_up)
    def _():
        pl.semaphore_signal(barrier, inc=1, device_id={"tp": peer[UP]}, device_id_type=MESH)

    @pl.when(has_down)
    def _():
        pl.semaphore_signal(barrier, inc=1, device_id={"tp": peer[DOWN]}, device_id_type=MESH)

    sub = lax.broadcasted_iota(jnp.int32, (row_count, 128), 0)
    place = jnp.zeros((row_count, 128), jnp.int32)
    code = jnp.zeros((row_count, 128), jnp.int32)
    for r in range(row_count):
        place = jnp.where(sub == r, place_ref[r], place)
    for b in range(page_count):
        dest = jnp.int32(0)
        for q in range(dest_ref.shape[0]):
            dest = dest + jnp.where(request_ref[b] == q, dest_ref[q], 0)
        code = jnp.where(sub // page_len == b, dest * slots + slot_ref[b], code)
    meta[me, 0] = place
    meta[me, 1] = code

    loads[0].wait()
    loads[1].wait()
    inv_rms = []
    for layer in range(layers):
        square = jnp.zeros((row_count, 128), jnp.float32)
        for j in range(model_dim // 128):
            values = hidden[layer, :, j * 128:(j + 1) * 128].astype(jnp.float32)
            square = square + values * values
        mean = jnp.sum(square, axis=1, keepdims=True) * (1.0 / model_dim)
        inv_rms.append(lax.rsqrt(mean + EPSILON))

    pl.semaphore_wait(barrier, 2 + has_up.astype(jnp.int32) + has_down.astype(jnp.int32))

    def copies(c, block, way):
        made = [
            pltpu.make_async_remote_copy(
                src_ref=rows.at[c, block], dst_ref=rows.at[c, block],
                send_sem=send_sem.at[way, c, block], recv_sem=recv_sem.at[c, block],
                device_id={"tp": peer[way]}, device_id_type=MESH,
            )
        ]
        if c == 0:
            made.append(
                pltpu.make_async_remote_copy(
                    src_ref=meta.at[block], dst_ref=meta.at[block],
                    send_sem=meta_send.at[way, block], recv_sem=meta_recv.at[block],
                    device_id={"tp": peer[way]}, device_id_type=MESH,
                )
            )
        return made

    def send(c, block, way):
        for copy in copies(c, block, way):
            copy.start()

    def receive(c, block):
        for copy in copies(c, block, Y):
            copy.wait_recv()

    both = ((UP, has_up), (DOWN, has_down))

    def hops(c):
        found = []
        for step in range(1, line):
            low, high = z >= step, z + step < line
            if c < crossed:
                found += [
                    (step, low, me - 2 * step, both[:1]),
                    (step, high, me + 2 * step, both[1:]),
                    (step + 1, low, peer[Y] - 2 * step, both[:1]),
                    (step + 1, high, peer[Y] + 2 * step, both[1:]),
                ]
            else:
                found += [
                    (step, low, me - 2 * step, both[:1] + ((Y, None),)),
                    (step, high, me + 2 * step, both[1:] + ((Y, None),)),
                ]
        if c < crossed:
            found.append((1, None, peer[Y], both))
        return found

    def guarded(cond, act):
        if cond is None:
            act()
        else:
            pl.when(cond)(act)

    def onward(act, c, block, ways):
        for way, cond in ways:
            guarded(cond, functools.partial(act, c, block, way))

    def send_own(c):
        span = slice(c * depth, (c + 1) * depth)
        normed = [
            hidden[layer, :, span].astype(jnp.float32) * inv_rms[layer] * gain[layer:layer + 1, span]
            for layer in range(layers)
        ]
        rows[c, me] = jnp.concatenate(normed, axis=0).astype(jnp.bfloat16)
        onward(send, c, me, both + ((Y, None),))

    def forward(c, block, ways):
        receive(c, block)
        onward(send, c, block, ways)

    tokens = team * row_count
    places = page_len * slots

    pair_code = pltpu.make_async_remote_copy(
        src_ref=meta, dst_ref=far_code, send_sem=pair_send.at[0], recv_sem=pair_recv.at[0],
        device_id={"inst": 1 - inst}, device_id_type=MESH,
    )

    def tables():
        position = meta[:, 0].reshape(tokens, 128).astype(jnp.float32)
        for g in range(wide // 128):
            if width % (2 * HD) == 0 and g % 2:
                continue
            column = me * width + g * 128 + lax.broadcasted_iota(jnp.int32, (1, 128), 1)
            freq = (column % HD // 2).astype(jnp.float32)
            angle = position * jnp.exp(-(2.0 * freq / HD) * math.log(ROPE_BASE))
            is_key = column % (2 * HD) < HD
            lanes = slice(g * 128, (g + 1) * 128)
            cos_ref[:, lanes] = jnp.where(is_key, jnp.cos(angle), 1.0)
            sine = jnp.where(is_key, jnp.sin(angle), 0.0)
            sin_ref[:, lanes] = jnp.where(column % 2 == 0, -sine, sine)

    def picks(side, source):
        code = source[:, 1].reshape(tokens, 128)[:, 0:1]
        spot = lax.broadcasted_iota(jnp.int32, (tokens, places), 1)
        token = lax.broadcasted_iota(jnp.int32, (tokens, places), 0)
        hit = (code == inst * slots + spot % slots) & (token % page_len == spot // slots)
        pick[side] = jnp.where(hit, 1.0, 0.0).T.astype(jnp.bfloat16)

    def multiply(c, fresh):
        block = rows[c].reshape(team * layers * row_count, depth)
        for layer in range(layers):
            part = lax.dot_general(
                block, weight[layer, :, c * depth:(c + 1) * depth],
                (((1,), (1,)), ((), ())), preferred_element_type=jnp.float32,
            )
            if fresh:
                total[layer, :, :width] = part
            else:
                total[layer, :, :width] += part

    if wide != width:
        total[...] = jnp.zeros_like(total)
    gap = GAP or chunks
    events = []
    for c in range(chunks):
        events.append((max(0, c - LOOKAHEAD), 0, len(events), functools.partial(send_own, c)))
        for stage, cond, block, ways in hops(c):
            act = functools.partial(guarded, cond, functools.partial(forward, c, block, ways))
            events.append((c + gap * stage, 1, len(events), act))

    first = crossed if crossed < chunks else 0

    def finish(c):
        if c >= crossed:
            for far in range(line):
                receive(c, 2 * far + 1 - y)
        if c == first:
            loads[2].wait()
            loads[3].wait()
        multiply(c, c == first)
        if c == 0:
            pair_code.start()
            tables()
            picks(0, meta)
        if c == min(1, chunks - 1):
            pair_code.wait_recv()
            picks(1, far_code)

    for c in range(chunks):
        events.append((max(c + gap * line, c + gap * (line + 1) if c < crossed else 0), 2, len(events), functools.partial(finish, c)))
    for event in sorted(events, key=lambda e: e[:3]):
        event[3]()

    lane = lax.broadcasted_iota(jnp.int32, (1, 128), 1)
    for layer in range(layers):
        acc = total[layer].reshape(team, layers * row_count, wide)
        acc = acc[:, layer * row_count:(layer + 1) * row_count].reshape(tokens, wide)
        for g in range(wide // 128):
            start, end = g * 128, min((g + 1) * 128, width)
            value = acc[:, g * 128:(g + 1) * 128]
            shift = bias[layer:layer + 1, start:end]
            if end - start < 128:
                shift = jnp.pad(shift, ((0, 0), (0, 128 - (end - start))))
            value = value + shift
            if not (width % (2 * HD) == 0 and g % 2):
                after = pltpu.roll(value, 127, 1)
                before = pltpu.roll(value, 1, 1)
                partner = jnp.where(lane % 2 == 0, after, before)
                value = value * cos_ref[:, start:start + 128] + partner * sin_ref[:, start:start + 128]
            turned[0, layer, :, g * 128:(g + 1) * 128] = value.astype(jnp.bfloat16)

    swap = pltpu.make_async_remote_copy(
        src_ref=turned.at[0], dst_ref=turned.at[1], send_sem=pair_send.at[1], recv_sem=pair_recv.at[1],
        device_id={"inst": 1 - inst}, device_id_type=MESH,
    )
    swap.start()
    near = [
        jnp.dot(pick[0], turned[0, layer], preferred_element_type=jnp.float32) for layer in range(layers)
    ]
    swap.wait_recv()
    for layer in range(layers):
        paged = near[layer] + jnp.dot(pick[1], turned[1, layer], preferred_element_type=jnp.float32)
        paged = paged.astype(jnp.bfloat16)
        for r in range(page_len):
            page_rows = paged[r * slots:(r + 1) * slots]
            if out_ref.ndim == 3:
                out_ref[layer, :, r * width:(r + 1) * width] = page_rows
            else:
                out_ref[layer, r] = page_rows

    def sent(c, block, way):
        for copy in copies(c, block, way):
            copy.wait_send()

    pair_code.wait_send()
    swap.wait_send()
    for c in range(chunks):
        onward(sent, c, me, ((Y, None),) + both)
        for _, cond, block, ways in hops(c):
            guarded(cond, functools.partial(onward, sent, c, block, ways))


def body(hidden, norm_gain, kv_weight, kv_bias, block_request, request_dest, block_slot, positions):
    layers, row_count, model_dim = hidden.shape
    page_count = block_request.shape[0]
    page_len = row_count // page_count
    width = kv_weight.shape[1]
    inst_count = lax.axis_size("inst")
    team = lax.axis_size("tp")
    slots = inst_count * team * page_count
    wide = -(-width // 128) * 128
    chunks = max(1, 32 // team)
    depth = model_dim // chunks
    tokens = team * row_count
    line = team // 2
    if wide == width:
        shape = (layers, slots, page_len * width)
    else:
        shape = (layers, page_len, slots, wide)
    smem = pl.BlockSpec(memory_space=pltpu.SMEM)
    anywhere = pl.BlockSpec(memory_space=pl.ANY)
    dma = pltpu.SemaphoreType.DMA
    out = pl.pallas_call(
        functools.partial(kernel, team, chunks, chunks // 8, page_len, page_count, slots),
        out_shape=jax.ShapeDtypeStruct(shape, jnp.bfloat16),
        in_specs=[smem] * 4 + [anywhere] * 4,
        out_specs=pl.BlockSpec(memory_space=pltpu.VMEM),
        scratch_shapes=[
            pltpu.VMEM((layers, row_count, model_dim), jnp.bfloat16),
            pltpu.VMEM((layers, model_dim), jnp.float32),
            pltpu.VMEM((layers, width, model_dim), jnp.bfloat16),
            pltpu.VMEM((layers, width), jnp.float32),
            pltpu.VMEM((chunks, team, layers * row_count, depth), jnp.bfloat16),
            pltpu.VMEM((team, 2, row_count, 128), jnp.int32),
            pltpu.VMEM((team, 2, row_count, 128), jnp.int32),
            pltpu.VMEM((layers, team * layers * row_count, wide), jnp.float32),
            pltpu.VMEM((2, layers, tokens, wide), jnp.bfloat16),
            pltpu.VMEM((tokens, wide), jnp.float32),
            pltpu.VMEM((tokens, wide), jnp.float32),
            pltpu.VMEM((2, page_len * slots, tokens), jnp.bfloat16),
            dma((4,)),
            dma((3, chunks, team)),
            dma((chunks, team)),
            dma((3, team)),
            dma((team,)),
            dma((2,)),
            dma((2,)),
        ],
        compiler_params=pltpu.CompilerParams(
            collective_id=0, has_side_effects=True, vmem_limit_bytes=62 * 1024 * 1024
        ),
        cost_estimate=pl.CostEstimate(
            flops=4 * layers * tokens * width * model_dim,
            bytes_accessed=2 * layers * width * model_dim,
            transcendentals=0,
        ),
        name="restore",
    )(block_request, request_dest, block_slot, positions, hidden, norm_gain, kv_weight, kv_bias)
    if wide != width:
        out = out[..., :width].transpose(0, 2, 1, 3)
    return out.reshape(layers, slots, 1, page_len * width)


def solution(mesh):
    placed = (
        P(None, ("group", "inst", "tp"), None),
        P(),
        P(None, "tp", None),
        P(None, "tp"),
        P(("group", "inst", "tp")),
        P("group"),
        P(("group", "inst", "tp")),
        P(("group", "inst", "tp")),
    )
    return jax.shard_map(
        body,
        mesh=mesh,
        in_specs=placed,
        out_specs=P(None, ("group", "inst"), "tp", None),
        check_vma=False,
    )
```
